32 devices in a mesh: leaf: 8 (over y, x, core), grid: 4 (over z).
Axes of the slice: x: 2, y: 2, z: 4, core: 2. Of those that a mesh axis runs over, the one named last changes fastest.
Arguments:
- child_front: float32 [8, 1, 2048, 4, 4, 128], P('leaf', None, None, None, 'grid'), as said below
- child_live: int32 [8, 1, 16], replicated, may hold values 0 or 1
- child_map: int32 [8, 1, 8], replicated, may hold values from 0 to 15, as said below
- parent_owner: int32 [4, 16], replicated, may hold values from 0 to 15, as said below
- parent_shift: float32 [8, 1, 2, 4, 128], P('leaf', None, None, 'grid'), may hold values from 0.5 to 2
Outputs:
- child_factor: float32 [8, 1, 2048, 2, 4, 128], P('leaf', None, None, None, 'grid')
- parent_done: float32 [8, 1, 2048, 2, 4, 128], P('leaf', None, None, None, 'grid')
The draws below stay inside these ranges and needn't reach their ends.
Inputs may be any that keep to these rules, and one draw needn't show every extreme that they name: `child_map`: each row holds 8 different block numbers in increasing order, the last one being 15. `parent_owner`: each row is a permutation of the 16 slots. `child_front`: each front is symmetric positive definite.
All inputs are finite; a program needn't handle non-finite values.
Results may differ from the reference program's by a relative error of at most 0.0003.
Values sent between devices are 32-bit elements; how exact they have to be, the bound alone decides.
A program may use at most 128 MiB of HBM per device.

```python
import math
import jax
import jax.numpy as jnp
from jax import lax

F = 2048
PIVOTS = 1024
NB = 128
FRONTS_DEV = 1
FB = 16
PB = 8
CB = 8
POS = 8
PAIRS = 4
T1 = 4
TP = 2
T2 = 2
N_GRID = 4


def draw_child_front(key, part):
    count = POS * FRONTS_DEV
    factor = jax.random.normal(jax.random.fold_in(key, 11), (count, F, F), jnp.float32)
    gram = jnp.einsum('pik,pjk->pij', factor, factor, precision=lax.Precision.HIGHEST) / F
    gram = 0.5 * (gram + jnp.swapaxes(gram, 1, 2))
    shift = jax.random.uniform(jax.random.fold_in(key, 13), (count, F), jnp.float32, 0.5, 1.5)
    matrix = gram + shift[:, :, None] * jnp.eye(F, dtype=jnp.float32)[None]
    return matrix.reshape(POS, FRONTS_DEV, F, T1, F // (NB * T1), NB)


def draw_child_map(key, part):
    count = POS * FRONTS_DEV
    keys = jax.random.split(jax.random.fold_in(key, 21), count)
    orders = jax.vmap(lambda single: jax.random.permutation(single, FB - 1))(keys)
    chosen = jnp.sort(orders[:, :CB - 1].astype(jnp.int32), axis=1)
    closing = jnp.full((count, 1), FB - 1, jnp.int32)
    return jnp.concatenate([chosen, closing], axis=1).reshape(POS, FRONTS_DEV, CB)


def draw_parent_owner(key, part):
    keys = jax.random.split(jax.random.fold_in(key, 31), PAIRS)
    return jax.vmap(lambda single: jax.random.permutation(single, FB))(keys).astype(jnp.int32)


def place_ends(values, key, low, largest):
    shape = values.shape
    spot = [jax.random.randint(jax.random.fold_in(key, axis), (), 0, shape[axis]) for axis in range(len(shape))]
    values = values.at[tuple(spot)].set(low)
    longest = shape.index(max(shape))
    spot[longest] = (spot[longest] + 1) % shape[longest]
    return values.at[tuple(spot)].set(largest)


def level_of(stream_key, extent, cuts, least, top_value):
    def one(dim, parts):
        steps = jax.random.uniform(jax.random.fold_in(jax.random.fold_in(stream_key, 6), dim), (parts,), jnp.float32, least / len(cuts), top_value / len(cuts))
        return jnp.repeat(jnp.exp(steps), extent[dim] // parts).reshape((-1,) + (1,) * (len(extent) - dim - 1))

    loudness = one(*cuts[0])
    for cut in cuts[1:]:
        loudness = loudness * one(*cut)
    return loudness


def setup_inputs(seed: int = 0) -> dict:
    seeds = jax.random.split(jax.random.key(seed), 6)
    return {
        "child_front": draw_child_front(jax.random.fold_in(seeds[5], 71), 0),
        "child_live": place_ends((jax.random.randint(seeds[1], (POS, FRONTS_DEV, FB), 0, 4) < 3).astype(jnp.int32), jax.random.fold_in(seeds[1], 1), 0, 1),
        "child_map": draw_child_map(jax.random.fold_in(seeds[5], 71), 0),
        "parent_owner": draw_parent_owner(jax.random.fold_in(seeds[5], 71), 0),
        "parent_shift": jnp.clip(jnp.exp(math.log(2.0) - 1.3862944 * jax.random.uniform(seeds[4], (POS, FRONTS_DEV, T2, N_GRID, NB), jnp.float32) ** level_of(seeds[4], (POS, FRONTS_DEV, T2, N_GRID, NB), ((0, 8), (3, 4)), -0.2, 0.2)), 0.5, 2.0),
    }


highest = lax.Precision.HIGHEST

def partial_factor(matrix):
    lower_part = jnp.linalg.cholesky(matrix[:PIVOTS, :PIVOTS])
    below_part = lax.linalg.triangular_solve(lower_part, matrix[PIVOTS:, :PIVOTS], left_side=False, lower=True, transpose_a=True)
    schur = matrix[PIVOTS:, PIVOTS:] - jnp.dot(below_part, below_part.T, precision=highest)
    return (jnp.concatenate([lower_part, below_part], axis=0), schur)

def assemble_child(entries, alive):
    matrix = entries.reshape(F, F)
    live_rows = jnp.repeat(alive.astype(jnp.float32), NB)
    identity = jnp.eye(F, dtype=jnp.float32)
    return matrix * live_rows[:, None] * live_rows[None, :] + identity * (1.0 - live_rows)[:, None]

def extend_schur(schur, targets, alive):
    place = (targets[None, :] == jnp.arange(FB, dtype=jnp.int32)[:, None]).astype(jnp.float32)
    place = place * alive.astype(jnp.float32)[None, :]
    tiles = schur.reshape(CB, NB, CB, NB)
    rows_done = jnp.einsum('bc,cidj->bidj', place, tiles, precision=highest)
    both_done = jnp.einsum('bidj,ed->bie j'.replace(' ', ''), rows_done, place, precision=highest)
    return both_done.reshape(F, F)

def reference(child_front, child_live, child_map, parent_owner, parent_shift):
    grid_count = F // (NB * T1)
    child_rows = []
    schurs = []
    for position in range(POS):
        factor_row = []
        schur_row = []
        for front_id in range(FRONTS_DEV):
            matrix = assemble_child(child_front[position, front_id], child_live[position, front_id])
            factor, schur = partial_factor(matrix)
            factor_row.append(factor.reshape(F, TP, grid_count, NB))
            schur_row.append(schur)
        child_rows.append(jnp.stack(factor_row))
        schurs.append(schur_row)
    child_factor = jnp.stack(child_rows)
    parent_rows = [[None] * FRONTS_DEV for position in range(POS)]
    for pair in range(PAIRS):
        owner = parent_owner[pair]
        for front_id in range(FRONTS_DEV):
            slot_shift = jnp.stack([parent_shift[2 * pair + member, front_id] for member in range(2)])
            slot_shift = jnp.transpose(slot_shift, (0, 2, 1, 3)).reshape(FB, NB)
            matrix = jnp.diag(slot_shift[owner].reshape(F))
            for member in range(2):
                child = 2 * pair + member
                matrix = matrix + extend_schur(schurs[child][front_id], child_map[child, front_id], child_live[child, front_id, PB:])
            factor, schur = partial_factor(matrix)
            finished = jnp.zeros((F, F), jnp.float32).at[:, :PIVOTS].set(factor).at[PIVOTS:, PIVOTS:].set(schur)
            slots = jnp.zeros((F, FB, NB), jnp.float32).at[:, owner, :].set(finished.reshape(F, FB, NB))
            slots = jnp.transpose(slots.reshape(F, 2, grid_count, T2, NB), (1, 0, 3, 2, 4))
            for member in range(2):
                parent_rows[2 * pair + member][front_id] = slots[member]
    parent_done = jnp.stack([jnp.stack(row) for row in parent_rows])
    return (child_factor, parent_done)
```

```python
import functools

import jax
import jax.numpy as jnp
from jax import lax
from jax.experimental import pallas as pl
from jax.experimental.pallas import tpu as pltpu
from jax.sharding import PartitionSpec as P

F = 2048
PIVOTS = 1024
NB = 128
FB = 16
PB = 8
CB = 8
CHUNK = 512
PAIR = 256
f32 = jnp.float32
bf16 = jnp.bfloat16
NT = (((1,), (1,)), ((), ()))
VMEM = pl.BlockSpec(memory_space=pltpu.VMEM)
SMEM = pl.BlockSpec(memory_space=pltpu.SMEM)
LIMIT = 56 * 1024 * 1024


def split(value):
    high = value.astype(bf16)
    return high, (value - high.astype(f32)).astype(bf16)


def times(a_high, a_low, b_high, b_low):
    def dot(a, b):
        return lax.dot_general(a, b, NT, preferred_element_type=f32)

    return dot(a_high, b_high) + (dot(a_low, b_high) + dot(a_high, b_low))


def rows_of(index, count):
    return pl.ds(pl.multiple_of(index * count, count), count)


def block_inverse(block_ref, inverse_ref):
    lane = lax.broadcasted_iota(jnp.int32, (8, NB), 1)
    sub = lax.broadcasted_iota(jnp.int32, (8, NB), 0)
    groups = NB // 8
    left = [block_ref[8 * g : 8 * g + 8, :] for g in range(groups)]
    right = [jnp.where(lane == sub + 8 * g, 1.0, 0.0).astype(f32) for g in range(groups)]
    for step in range(NB):
        g, j = divmod(step, 8)
        column = jnp.broadcast_to(left[g][:, step : step + 1], (8, NB))
        pivot = jnp.broadcast_to(column[j : j + 1, :], (8, NB))
        scale = 1.0 / pivot
        row_left = jnp.broadcast_to(left[g][j : j + 1, :], (8, NB)) * scale
        row_right = jnp.broadcast_to(right[g][j : j + 1, :], (8, NB)) * scale
        diagonal = pivot if j == 0 else jnp.where(sub >= j, pivot, diagonal)
        if j < 7:
            below = jnp.where(sub > j, column, 0.0)
            left[g] = left[g] - below * row_left
            right[g] = right[g] - below * row_right
        for v in range(g + 1, groups):
            column = jnp.broadcast_to(left[v][:, step : step + 1], (8, NB))
            left[v] = left[v] - column * row_left
            right[v] = right[v] - column * row_right
        if j == 7:
            inverse_ref[8 * g : 8 * g + 8, :] = right[g] * lax.rsqrt(diagonal)


def factor_blocks(front, high, low, block, inverse, count, height, emit):
    chunks = height // CHUNK
    block[...] = front[0, 0:NB, 0:NB]

    def solve(panel, pair, first):
        cols = slice(first, first + NB)
        inv_high, inv_low = split(inverse[...])

        def one(k, carry):
            rows = rows_of(k, CHUNK)
            value = times(*split(front[pair, rows, cols]), inv_high, inv_low)
            place = lax.broadcasted_iota(jnp.int32, (CHUNK, NB), 0) + (k * CHUNK - panel * NB)
            value = jnp.where(place >= lax.broadcasted_iota(jnp.int32, (CHUNK, NB), 1), value, 0.0)
            value_high, value_low = split(value)
            high[pair, rows, cols] = value_high
            low[pair, rows, cols] = value_low
            emit(panel, rows, value)
            return carry

        lax.fori_loop(panel * NB // CHUNK, chunks, one, 0)

    def step(panel, carry):
        pair = panel // 2
        block_inverse(block, inverse)

        @pl.when(panel % 2 == 0)
        def _():
            solve(panel, pair, 0)
            next_rows = rows_of(panel + 1, NB)
            part_high = high[pair, next_rows, 0:NB]
            part_low = low[pair, next_rows, 0:NB]

            def one(k, carry):
                rows = rows_of(k, CHUNK)
                front[pair, rows, NB:PAIR] -= times(
                    high[pair, rows, 0:NB], low[pair, rows, 0:NB], part_high, part_low
                )
                return carry

            lax.fori_loop(panel * NB // CHUNK, chunks, one, 0)
            block[...] = front[pair, next_rows, NB:PAIR]

        @pl.when(panel % 2 == 1)
        def _():
            solve(panel, pair, NB)

            def column(q, carry):
                part_high = high[pair, rows_of(q, PAIR), :]
                part_low = low[pair, rows_of(q, PAIR), :]

                def one(k, carry):
                    rows = rows_of(k, CHUNK)
                    front[q, rows, :] -= times(high[pair, rows, :], low[pair, rows, :], part_high, part_low)
                    return carry

                lax.fori_loop(q * PAIR // CHUNK, chunks, one, 0)
                return carry

            lax.fori_loop(pair + 1, count // 2, column, 0)

            @pl.when(pair + 1 < count // 2)
            def _():
                block[...] = front[pair + 1, rows_of(panel + 1, NB), 0:NB]

        return carry

    lax.fori_loop(0, count, step, 0)


def masked(value, live_row, live_col, same):
    row = lax.broadcasted_iota(jnp.int32, (NB, NB), 0)
    col = lax.broadcasted_iota(jnp.int32, (NB, NB), 1)
    kept = jnp.where(live_row * live_col > 0, value, 0.0)
    alone = jnp.where(same & (live_row == 0), 1.0, 0.0)
    return kept + jnp.where(row == col, alone, 0.0)


def child_kernel(index, grid_count, live, place, entries, *rest):
    done = rest[: 2 * index]
    own, high, low, front, block, inverse = rest[2 * index :]
    base = index * grid_count * NB
    height = F - base
    own[...] = jnp.zeros_like(own)

    def load(q, carry):
        for half in range(2):
            col = 2 * q + half
            live_col = live[index * grid_count + col]
            for r in range(height // NB):
                front[q, r * NB : (r + 1) * NB, half * NB : (half + 1) * NB] = masked(
                    entries[col, r * NB : (r + 1) * NB, :], live[base // NB + r], live_col, col == r
                )
        return carry

    lax.fori_loop(0, grid_count // 2, load, 0)
    for earlier in range(index):
        past_high, past_low = done[2 * earlier], done[2 * earlier + 1]
        offset = (index - earlier) * grid_count * NB

        def column(q, carry):
            def pairs(p, carry):
                near = pl.ds(pl.multiple_of(offset + q * PAIR, PAIR), PAIR)
                part_high, part_low = past_high[p, near, :], past_low[p, near, :]

                def one(k, carry):
                    rows = pl.ds(pl.multiple_of(offset + k * CHUNK, CHUNK), CHUNK)
                    front[q, rows_of(k, CHUNK), :] -= times(
                        past_high[p, rows, :], past_low[p, rows, :], part_high, part_low
                    )
                    return carry

                return lax.fori_loop(q * PAIR // CHUNK, height // CHUNK, one, carry)

            return lax.fori_loop(0, grid_count // 2, pairs, carry)

        lax.fori_loop(0, grid_count // 2, column, 0)

    def emit(panel, rows, value):
        @pl.when(panel == place[0])
        def _():
            own[pl.ds(pl.multiple_of(rows.start + base, NB), rows.size), :] = value

    factor_blocks(front, high, low, block, inverse, grid_count, height, emit)


def schur_kernel(rounds, pivot_rounds, grid_count, live, *rest):
    late = rounds - pivot_rounds
    entries = rest[:late]
    done = rest[late : late + 2 * pivot_rounds]
    (out,) = rest[late + 2 * pivot_rounds :]
    for q in range(CB // 2):
        source = 2 * q // grid_count
        inner = 2 * q % grid_count
        shift = source * grid_count * NB

        def tile(k, carry):
            total = None
            for index in range(pivot_rounds):
                past_high, past_low = done[2 * index], done[2 * index + 1]
                offset = PIVOTS - index * grid_count * NB
                rows = pl.ds(pl.multiple_of(offset + k * PAIR, PAIR), PAIR)
                near = slice(offset + q * PAIR, offset + (q + 1) * PAIR)
                for p in range(grid_count // 2):
                    product = times(
                        past_high[p, rows, :], past_low[p, rows, :], past_high[p, near, :], past_low[p, near, :]
                    )
                    total = product if total is None else total + product
            for row in range(2):
                for col in range(2):
                    r = 2 * k + row
                    c = 2 * q + col
                    value = entries[source][inner + col, pl.ds(pl.multiple_of(r * NB - shift, NB), NB), :]
                    value = masked(value, live[PB + r], live[PB + c], r == c)
                    part = total[row * NB : (row + 1) * NB, col * NB : (col + 1) * NB]
                    out[c, rows_of(r, NB), :] = value - part
            return carry

        lax.fori_loop(q, CB // 2, tile, 0)


def parent_kernel(slots, blocks, mine_at, other_at, mine, other, diagonal, own, front, high, low, block, inverse):
    row_id = lax.broadcasted_iota(jnp.int32, (NB, NB), 0)
    col_id = lax.broadcasted_iota(jnp.int32, (NB, NB), 1)
    own[...] = jnp.zeros_like(own)

    def extension(schur, at, r, b, turn):
        cr, cb = at[r], at[b]
        present = (cr >= 0) & (cb >= 0)
        cr, cb = jnp.maximum(cr, 0), jnp.maximum(cb, 0)
        if not turn:
            value = schur[cb, rows_of(cr, NB), :]
        else:
            value = schur[jnp.minimum(cr, cb), rows_of(jnp.maximum(cr, cb), NB), :]
            value = jnp.where(cr >= cb, value, value.T)
        return jnp.where(present, value, 0.0)

    def assembled(r, b, turn):
        start = jnp.where((row_id == col_id) & (r == b), diagonal[pl.ds(b, 1), :], 0.0)
        return start + extension(mine, mine_at, r, b, turn) + extension(other, other_at, r, b, turn)

    def load(q, carry):
        for half in range(2):
            b = 2 * q + half

            def one(r, carry):
                front[q, rows_of(r, NB), half * NB : (half + 1) * NB] = assembled(r, b, False)
                return carry

            lax.fori_loop(b, FB, one, 0)
        return carry

    lax.fori_loop(0, PB // 2, load, 0)

    def emit(panel, rows, value):
        for s in range(slots):

            @pl.when(blocks[s] == panel)
            def _():
                own[s, rows, :] = value

    factor_blocks(front, high, low, block, inverse, PB, F, emit)

    def finish(s, carry):
        b = blocks[s]

        @pl.when(b >= PB)
        def _():
            def one(r, carry):
                own[s, rows_of(r, NB), :] = assembled(r, b, True)
                return carry

            lax.fori_loop(PB, FB, one, 0)
            near = rows_of(b, NB)

            def part(k, carry):
                rows = rows_of(k, CHUNK)
                total = None
                for p in range(PB // 2):
                    product = times(high[p, rows, :], low[p, rows, :], high[p, near, :], low[p, near, :])
                    total = product if total is None else total + product
                own[s, rows, :] -= total
                return carry

            lax.fori_loop(PIVOTS // CHUNK, F // CHUNK, part, 0)

        return carry

    lax.fori_loop(0, slots, finish, 0)


def call(kernel, outs, scratch, smem, vmem, flops):
    size = sum(a.size * a.dtype.itemsize for a in vmem) + sum(a.size * a.dtype.itemsize for a in outs)
    return pl.pallas_call(
        kernel,
        out_shape=outs,
        in_specs=[SMEM] * len(smem) + [VMEM] * len(vmem),
        out_specs=[VMEM] * len(outs),
        scratch_shapes=scratch,
        compiler_params=pltpu.CompilerParams(vmem_limit_bytes=LIMIT),
        cost_estimate=pl.CostEstimate(flops=flops, bytes_accessed=size, transcendentals=0),
    )(*smem, *vmem)


def shape(dims, dtype=f32):
    return jax.ShapeDtypeStruct(dims, dtype)


def body(child_front, child_live, child_map, parent_owner, parent_shift):
    grid_count = lax.axis_size("grid")
    leaf_count = lax.axis_size("leaf")
    grid_pos = lax.axis_index("grid")
    leaf_pos = lax.axis_index("leaf")
    member = leaf_pos % 2
    sibling = leaf_pos ^ 1
    rounds = child_front.shape[3]
    pivot_rounds = PIVOTS // (NB * grid_count)
    slots = parent_shift.shape[2]
    swap = [(source, source ^ 1) for source in range(leaf_count)]
    entries = child_front.reshape(F, rounds, NB)
    shifts = lax.all_gather(parent_shift.reshape(slots, NB), "grid", axis=0)
    gathered = [
        lax.all_gather(entries[t * grid_count * NB :, t, :], "grid", axis=0) for t in range(rounds)
    ]

    my_live = lax.dynamic_index_in_dim(child_live, leaf_pos, 0, keepdims=False)[0]
    other_live = lax.dynamic_index_in_dim(child_live, sibling, 0, keepdims=False)[0]
    my_map = lax.dynamic_index_in_dim(child_map, leaf_pos, 0, keepdims=False)[0]
    other_map = lax.dynamic_index_in_dim(child_map, sibling, 0, keepdims=False)[0]

    def sources(targets, alive):
        hit = (targets[None, :] == jnp.arange(FB)[:, None]) & (alive[None, PB:] > 0)
        return jnp.sum(jnp.where(hit, jnp.arange(1, CB + 1)[None, :], 0), axis=1).astype(jnp.int32) - 1

    owner_row = lax.dynamic_index_in_dim(parent_owner, leaf_pos // 2, 0, keepdims=False)
    slot_ids = (member * grid_count + grid_pos) * slots + jnp.arange(slots)
    holders = (owner_row[:, None] == slot_ids[None, :]).astype(jnp.int32)
    parent_blocks = jnp.sum(holders * jnp.arange(FB)[:, None], axis=0).astype(jnp.int32)
    other_shifts = lax.ppermute(shifts, "leaf", swap)
    first = jnp.where(member == 0, shifts, other_shifts)
    second = jnp.where(member == 0, other_shifts, shifts)
    by_slot = jnp.concatenate([first, second], axis=0).reshape(FB, NB)
    chosen = owner_row[:, None, None] == jnp.arange(FB)[None, :, None]
    diagonal = jnp.sum(jnp.where(chosen, by_slot[None], 0.0), axis=1)

    place = grid_pos.astype(jnp.int32).reshape(1)
    owned = []
    done = []
    for t in range(pivot_rounds):
        height = F - t * grid_count * NB
        packed = (grid_count // 2, height, PAIR)
        own, high, low = call(
            functools.partial(child_kernel, t, grid_count),
            [shape((F, NB)), shape(packed, bf16), shape(packed, bf16)],
            [pltpu.VMEM(packed, f32), pltpu.VMEM((NB, NB), f32), pltpu.VMEM((NB, NB), f32)],
            [my_live, place],
            [gathered[t], *done],
            25_000_000_000,
        )
        owned.append(own)
        done += [high, low]
    (mine,) = call(
        functools.partial(schur_kernel, rounds, pivot_rounds, grid_count),
        [shape((CB, F - PIVOTS, NB))],
        [],
        [my_live],
        [*gathered[pivot_rounds:], *done],
        6_000_000_000,
    )
    other = lax.ppermute(mine, "leaf", swap)
    packed = (PB // 2, F, PAIR)
    (parent,) = call(
        functools.partial(parent_kernel, slots),
        [shape((slots, F, NB))],
        [
            pltpu.VMEM(packed, f32),
            pltpu.VMEM(packed, bf16),
            pltpu.VMEM(packed, bf16),
            pltpu.VMEM((NB, NB), f32),
            pltpu.VMEM((NB, NB), f32),
        ],
        [parent_blocks, sources(my_map, my_live), sources(other_map, other_live)],
        [mine, other, diagonal],
        50_000_000_000,
    )
    child_factor = jnp.stack(owned, axis=1)
    parent_done = jnp.swapaxes(parent, 0, 1)
    return (
        child_factor.reshape(1, 1, F, pivot_rounds, 1, NB),
        parent_done.reshape(1, 1, F, slots, 1, NB),
    )


def solution(mesh):
    in_specs = (
        P("leaf", None, None, None, "grid", None),
        P(),
        P(),
        P(),
        P("leaf", None, None, "grid", None),
    )
    out_specs = (
        P("leaf", None, None, None, "grid", None),
        P("leaf", None, None, None, "grid", None),
    )
    return jax.shard_map(body, mesh=mesh, in_specs=in_specs, out_specs=out_specs, check_vma=False)
```

```python
import functools

import jax
import jax.numpy as jnp
from jax import lax
from jax.experimental import pallas as pl
from jax.experimental.pallas import tpu as pltpu
from jax.sharding import PartitionSpec as P

F = 2048
PIVOTS = 1024
NB = 128
FB = 16
PB = 8
CB = 8
CHUNK = 512
PAIR = 256
f32 = jnp.float32
bf16 = jnp.bfloat16
NT = (((1,), (1,)), ((), ()))
VMEM = pl.BlockSpec(memory_space=pltpu.VMEM)
SMEM = pl.BlockSpec(memory_space=pltpu.SMEM)
LIMIT = 56 * 1024 * 1024


def split(value):
    high = value.astype(bf16)
    return high, (value - high.astype(f32)).astype(bf16)


def times(a_high, a_low, b_high, b_low):
    def dot(a, b):
        return lax.dot_general(a, b, NT, preferred_element_type=f32)

    return dot(a_high, b_high) + (dot(a_low, b_high) + dot(a_high, b_low))


def rows_of(index, count):
    return pl.ds(pl.multiple_of(index * count, count), count)


def block_inverse(block_ref, inverse_ref):
    lane = lax.broadcasted_iota(jnp.int32, (8, NB), 1)
    sub = lax.broadcasted_iota(jnp.int32, (8, NB), 0)
    groups = NB // 8
    left = [block_ref[8 * g : 8 * g + 8, :] for g in range(groups)]
    right = [jnp.where(lane == sub + 8 * g, 1.0, 0.0).astype(f32) for g in range(groups)]
    for g in range(groups):
        columns = [jnp.broadcast_to(left[g][:, 8 * g + i : 8 * g + i + 1], (8, NB)) for i in range(8)]
        rows_left, rows_right = left[g], right[g]
        diagonal = solved = None
        for i in range(8):
            pivot = jnp.broadcast_to(columns[i][i : i + 1, :], (8, NB))
            factor = jnp.where(sub == i, 0.0, columns[i]) * (1.0 / pivot)
            for c in range(i + 1, 8):
                columns[c] = columns[c] - factor * jnp.broadcast_to(columns[c][i : i + 1, :], (8, NB))
            row_right = jnp.broadcast_to(rows_right[i : i + 1, :], (8, NB))
            diagonal = pivot if i == 0 else jnp.where(sub == i, pivot, diagonal)
            solved = row_right if i == 0 else jnp.where(sub == i, row_right, solved)
            rows_left = rows_left - factor * jnp.broadcast_to(rows_left[i : i + 1, :], (8, NB))
            rows_right = rows_right - factor * row_right
        inverse_ref[8 * g : 8 * g + 8, :] = solved * lax.rsqrt(diagonal)
        if g + 1 == groups:
            break
        over = 1.0 / diagonal
        rows_left, rows_right = rows_left * over, rows_right * over
        spread_left = [jnp.broadcast_to(rows_left[i : i + 1, :], (8, NB)) for i in range(8)]
        spread_right = [jnp.broadcast_to(rows_right[i : i + 1, :], (8, NB)) for i in range(8)]
        for v in range(g + 1, groups):
            factors = [jnp.broadcast_to(left[v][:, 8 * g + i : 8 * g + i + 1], (8, NB)) for i in range(8)]
            for i in range(8):
                left[v] = left[v] - factors[i] * spread_left[i]
                right[v] = right[v] - factors[i] * spread_right[i]


def factor_blocks(front, high, low, block, inverse, count, height, emit):
    chunks = height // CHUNK
    block[...] = front[0, 0:NB, 0:NB]

    def solve(panel, pair, first):
        cols = slice(first, first + NB)
        inv_high, inv_low = split(inverse[...])

        def one(k, carry):
            rows = rows_of(k, CHUNK)
            value = times(*split(front[pair, rows, cols]), inv_high, inv_low)
            place = lax.broadcasted_iota(jnp.int32, (CHUNK, NB), 0) + (k * CHUNK - panel * NB)
            value = jnp.where(place >= lax.broadcasted_iota(jnp.int32, (CHUNK, NB), 1), value, 0.0)
            value_high, value_low = split(value)
            high[pair, rows, cols] = value_high
            low[pair, rows, cols] = value_low
            emit(panel, rows, value)
            return carry

        lax.fori_loop(panel * NB // CHUNK, chunks, one, 0)

    def step(panel, carry):
        pair = panel // 2
        block_inverse(block, inverse)

        @pl.when(panel % 2 == 0)
        def _():
            solve(panel, pair, 0)
            next_rows = rows_of(panel + 1, NB)
            part_high = high[pair, next_rows, 0:NB]
            part_low = low[pair, next_rows, 0:NB]

            def one(k, carry):
                rows = rows_of(k, CHUNK)
                front[pair, rows, NB:PAIR] -= times(
                    high[pair, rows, 0:NB], low[pair, rows, 0:NB], part_high, part_low
                )
                return carry

            lax.fori_loop(panel * NB // CHUNK, chunks, one, 0)
            block[...] = front[pair, next_rows, NB:PAIR]

        @pl.when(panel % 2 == 1)
        def _():
            solve(panel, pair, NB)

            def column(q, carry):
                part_high = high[pair, rows_of(q, PAIR), :]
                part_low = low[pair, rows_of(q, PAIR), :]

                def one(k, carry):
                    rows = rows_of(k, CHUNK)
                    front[q, rows, :] -= times(high[pair, rows, :], low[pair, rows, :], part_high, part_low)
                    return carry

                lax.fori_loop(q * PAIR // CHUNK, chunks, one, 0)
                return carry

            lax.fori_loop(pair + 1, count // 2, column, 0)

            @pl.when(pair + 1 < count // 2)
            def _():
                block[...] = front[pair + 1, rows_of(panel + 1, NB), 0:NB]

        return carry

    lax.fori_loop(0, count, step, 0)


def masked(value, live_row, live_col, same):
    row = lax.broadcasted_iota(jnp.int32, (NB, NB), 0)
    col = lax.broadcasted_iota(jnp.int32, (NB, NB), 1)
    kept = jnp.where(live_row * live_col > 0, value, 0.0)
    alone = jnp.where(same & (live_row == 0), 1.0, 0.0)
    return kept + jnp.where(row == col, alone, 0.0)


def child_kernel(index, grid_count, live, place, entries, *rest):
    done = rest[: 2 * index]
    own, high, low, front, block, inverse = rest[2 * index :]
    base = index * grid_count * NB
    height = F - base
    own[...] = jnp.zeros_like(own)

    def load(q, carry):
        for half in range(2):
            col = 2 * q + half
            live_col = live[index * grid_count + col]
            for r in range(height // NB):
                front[q, r * NB : (r + 1) * NB, half * NB : (half + 1) * NB] = masked(
                    entries[col, r * NB : (r + 1) * NB, :], live[base // NB + r], live_col, col == r
                )
        return carry

    lax.fori_loop(0, grid_count // 2, load, 0)
    for earlier in range(index):
        past_high, past_low = done[2 * earlier], done[2 * earlier + 1]
        offset = (index - earlier) * grid_count * NB

        def column(q, carry):
            def pairs(p, carry):
                near = pl.ds(pl.multiple_of(offset + q * PAIR, PAIR), PAIR)
                part_high, part_low = past_high[p, near, :], past_low[p, near, :]

                def one(k, carry):
                    rows = pl.ds(pl.multiple_of(offset + k * CHUNK, CHUNK), CHUNK)
                    front[q, rows_of(k, CHUNK), :] -= times(
                        past_high[p, rows, :], past_low[p, rows, :], part_high, part_low
                    )
                    return carry

                return lax.fori_loop(q * PAIR // CHUNK, height // CHUNK, one, carry)

            return lax.fori_loop(0, grid_count // 2, pairs, carry)

        lax.fori_loop(0, grid_count // 2, column, 0)

    def emit(panel, rows, value):
        @pl.when(panel == place[0])
        def _():
            own[pl.ds(pl.multiple_of(rows.start + base, NB), rows.size), :] = value

    factor_blocks(front, high, low, block, inverse, grid_count, height, emit)


def schur_kernel(rounds, pivot_rounds, grid_count, live, *rest):
    late = rounds - pivot_rounds
    entries = rest[:late]
    done = rest[late : late + 2 * pivot_rounds]
    (out,) = rest[late + 2 * pivot_rounds :]
    for q in range(CB // 2):
        source = 2 * q // grid_count
        inner = 2 * q % grid_count
        shift = source * grid_count * NB

        def tile(k, carry):
            total = None
            for index in range(pivot_rounds):
                past_high, past_low = done[2 * index], done[2 * index + 1]
                offset = PIVOTS - index * grid_count * NB
                rows = pl.ds(pl.multiple_of(offset + k * PAIR, PAIR), PAIR)
                near = slice(offset + q * PAIR, offset + (q + 1) * PAIR)
                for p in range(grid_count // 2):
                    product = times(
                        past_high[p, rows, :], past_low[p, rows, :], past_high[p, near, :], past_low[p, near, :]
                    )
                    total = product if total is None else total + product
            for row in range(2):
                for col in range(2):
                    r = 2 * k + row
                    c = 2 * q + col
                    value = entries[source][inner + col, pl.ds(pl.multiple_of(r * NB - shift, NB), NB), :]
                    value = masked(value, live[PB + r], live[PB + c], r == c)
                    part = total[row * NB : (row + 1) * NB, col * NB : (col + 1) * NB]
                    out[c, rows_of(r, NB), :] = value - part
            return carry

        lax.fori_loop(q, CB // 2, tile, 0)


def parent_kernel(slots, blocks, mine_at, other_at, mine, other, diagonal, own, front, high, low, block, inverse):
    row_id = lax.broadcasted_iota(jnp.int32, (NB, NB), 0)
    col_id = lax.broadcasted_iota(jnp.int32, (NB, NB), 1)
    own[...] = jnp.zeros_like(own)

    def extension(schur, at, r, b, turn):
        cr, cb = at[r], at[b]
        present = (cr >= 0) & (cb >= 0)
        cr, cb = jnp.maximum(cr, 0), jnp.maximum(cb, 0)
        if not turn:
            value = schur[cb, rows_of(cr, NB), :]
        else:
            value = schur[jnp.minimum(cr, cb), rows_of(jnp.maximum(cr, cb), NB), :]
            value = jnp.where(cr >= cb, value, value.T)
        return jnp.where(present, value, 0.0)

    def assembled(r, b, turn):
        start = jnp.where((row_id == col_id) & (r == b), diagonal[pl.ds(b, 1), :], 0.0)
        return start + extension(mine, mine_at, r, b, turn) + extension(other, other_at, r, b, turn)

    def load(q, carry):
        for half in range(2):
            b = 2 * q + half

            def one(r, carry):
                front[q, rows_of(r, NB), half * NB : (half + 1) * NB] = assembled(r, b, False)
                return carry

            lax.fori_loop(b, FB, one, 0)
        return carry

    lax.fori_loop(0, PB // 2, load, 0)

    def emit(panel, rows, value):
        for s in range(slots):

            @pl.when(blocks[s] == panel)
            def _():
                own[s, rows, :] = value

    factor_blocks(front, high, low, block, inverse, PB, F, emit)

    def finish(s, carry):
        b = blocks[s]

        @pl.when(b >= PB)
        def _():
            def one(r, carry):
                own[s, rows_of(r, NB), :] = assembled(r, b, True)
                return carry

            lax.fori_loop(PB, FB, one, 0)
            near = rows_of(b, NB)

            def part(k, carry):
                rows = rows_of(k, CHUNK)
                total = None
                for p in range(PB // 2):
                    product = times(high[p, rows, :], low[p, rows, :], high[p, near, :], low[p, near, :])
                    total = product if total is None else total + product
                own[s, rows, :] -= total
                return carry

            lax.fori_loop(PIVOTS // CHUNK, F // CHUNK, part, 0)

        return carry

    lax.fori_loop(0, slots, finish, 0)


def call(kernel, outs, scratch, smem, vmem, flops):
    size = sum(a.size * a.dtype.itemsize for a in vmem) + sum(a.size * a.dtype.itemsize for a in outs)
    return pl.pallas_call(
        kernel,
        out_shape=outs,
        in_specs=[SMEM] * len(smem) + [VMEM] * len(vmem),
        out_specs=[VMEM] * len(outs),
        scratch_shapes=scratch,
        compiler_params=pltpu.CompilerParams(vmem_limit_bytes=LIMIT),
        cost_estimate=pl.CostEstimate(flops=flops, bytes_accessed=size, transcendentals=0),
    )(*smem, *vmem)


def shape(dims, dtype=f32):
    return jax.ShapeDtypeStruct(dims, dtype)


def body(child_front, child_live, child_map, parent_owner, parent_shift):
    grid_count = lax.axis_size("grid")
    leaf_count = lax.axis_size("leaf")
    grid_pos = lax.axis_index("grid")
    leaf_pos = lax.axis_index("leaf")
    member = leaf_pos % 2
    sibling = leaf_pos ^ 1
    rounds = child_front.shape[3]
    pivot_rounds = PIVOTS // (NB * grid_count)
    slots = parent_shift.shape[2]
    swap = [(source, source ^ 1) for source in range(leaf_count)]
    entries = child_front.reshape(F, rounds, NB)
    shifts = lax.all_gather(parent_shift.reshape(slots, NB), "grid", axis=0)
    gathered = [
        lax.all_gather(entries[t * grid_count * NB :, t, :], "grid", axis=0) for t in range(rounds)
    ]

    my_live = lax.dynamic_index_in_dim(child_live, leaf_pos, 0, keepdims=False)[0]
    other_live = lax.dynamic_index_in_dim(child_live, sibling, 0, keepdims=False)[0]
    my_map = lax.dynamic_index_in_dim(child_map, leaf_pos, 0, keepdims=False)[0]
    other_map = lax.dynamic_index_in_dim(child_map, sibling, 0, keepdims=False)[0]

    def sources(targets, alive):
        hit = (targets[None, :] == jnp.arange(FB)[:, None]) & (alive[None, PB:] > 0)
        return jnp.sum(jnp.where(hit, jnp.arange(1, CB + 1)[None, :], 0), axis=1).astype(jnp.int32) - 1

    owner_row = lax.dynamic_index_in_dim(parent_owner, leaf_pos // 2, 0, keepdims=False)
    slot_ids = (member * grid_count + grid_pos) * slots + jnp.arange(slots)
    holders = (owner_row[:, None] == slot_ids[None, :]).astype(jnp.int32)
    parent_blocks = jnp.sum(holders * jnp.arange(FB)[:, None], axis=0).astype(jnp.int32)
    other_shifts = lax.ppermute(shifts, "leaf", swap)
    first = jnp.where(member == 0, shifts, other_shifts)
    second = jnp.where(member == 0, other_shifts, shifts)
    by_slot = jnp.concatenate([first, second], axis=0).reshape(FB, NB)
    chosen = owner_row[:, None, None] == jnp.arange(FB)[None, :, None]
    diagonal = jnp.sum(jnp.where(chosen, by_slot[None], 0.0), axis=1)

    gathered[0], diagonal = lax.optimization_barrier((gathered[0], diagonal))
    place = grid_pos.astype(jnp.int32).reshape(1)
    owned = []
    done = []
    for t in range(pivot_rounds):
        height = F - t * grid_count * NB
        packed = (grid_count // 2, height, PAIR)
        own, high, low = call(
            functools.partial(child_kernel, t, grid_count),
            [shape((F, NB)), shape(packed, bf16), shape(packed, bf16)],
            [pltpu.VMEM(packed, f32), pltpu.VMEM((NB, NB), f32), pltpu.VMEM((NB, NB), f32)],
            [my_live, place],
            [gathered[t], *done],
            25_000_000_000,
        )
        owned.append(own)
        done += [high, low]
    (mine,) = call(
        functools.partial(schur_kernel, rounds, pivot_rounds, grid_count),
        [shape((CB, F - PIVOTS, NB))],
        [],
        [my_live],
        [*gathered[pivot_rounds:], *done],
        6_000_000_000,
    )
    other = lax.ppermute(mine, "leaf", swap)
    packed = (PB // 2, F, PAIR)
    (parent,) = call(
        functools.partial(parent_kernel, slots),
        [shape((slots, F, NB))],
        [
            pltpu.VMEM(packed, f32),
            pltpu.VMEM(packed, bf16),
            pltpu.VMEM(packed, bf16),
            pltpu.VMEM((NB, NB), f32),
            pltpu.VMEM((NB, NB), f32),
        ],
        [parent_blocks, sources(my_map, my_live), sources(other_map, other_live)],
        [mine, other, diagonal],
        50_000_000_000,
    )
    child_factor = jnp.stack(owned, axis=1)
    parent_done = jnp.swapaxes(parent, 0, 1)
    return (
        child_factor.reshape(1, 1, F, pivot_rounds, 1, NB),
        parent_done.reshape(1, 1, F, slots, 1, NB),
    )


def solution(mesh):
    in_specs = (
        P("leaf", None, None, None, "grid", None),
        P(),
        P(),
        P(),
        P("leaf", None, None, "grid", None),
    )
    out_specs = (
        P("leaf", None, None, None, "grid", None),
        P("leaf", None, None, None, "grid", None),
    )
    return jax.shard_map(body, mesh=mesh, in_specs=in_specs, out_specs=out_specs, check_vma=False)
```

```python
import functools

import jax
import jax.numpy as jnp
from jax import lax
from jax.experimental import pallas as pl
from jax.experimental.pallas import tpu as pltpu
from jax.sharding import PartitionSpec as P

F = 2048
PIVOTS = 1024
NB = 128
FB = 16
PB = 8
CB = 8
CHUNK = 512
PAIR = 256
f32 = jnp.float32
bf16 = jnp.bfloat16
NT = (((1,), (1,)), ((), ()))
VMEM = pl.BlockSpec(memory_space=pltpu.VMEM)
SMEM = pl.BlockSpec(memory_space=pltpu.SMEM)
LIMIT = 56 * 1024 * 1024


def split(value):
    high = value.astype(bf16)
    return high, (value - high.astype(f32)).astype(bf16)


def times(a_high, a_low, b_high, b_low):
    def dot(a, b):
        return lax.dot_general(a, b, NT, preferred_element_type=f32)

    return dot(a_high, b_high) + (dot(a_low, b_high) + dot(a_high, b_low))


def rows_of(index, count):
    return pl.ds(pl.multiple_of(index * count, count), count)


def block_inverse(block_ref, inverse_ref):
    lane = lax.broadcasted_iota(jnp.int32, (8, NB), 1)
    sub = lax.broadcasted_iota(jnp.int32, (8, NB), 0)
    groups = NB // 8
    left = [block_ref[8 * g : 8 * g + 8, :] for g in range(groups)]
    right = [jnp.where(lane == sub + 8 * g, 1.0, 0.0).astype(f32) for g in range(groups)]
    for g in range(groups):
        columns = [jnp.broadcast_to(left[g][:, 8 * g + i : 8 * g + i + 1], (8, NB)) for i in range(8)]
        rows_left, rows_right = left[g], right[g]
        diagonal = solved = None
        for i in range(8):
            pivot = jnp.broadcast_to(columns[i][i : i + 1, :], (8, NB))
            factor = jnp.where(sub == i, 0.0, columns[i]) * (1.0 / pivot)
            for c in range(i + 1, 8):
                columns[c] = columns[c] - factor * jnp.broadcast_to(columns[c][i : i + 1, :], (8, NB))
            row_right = jnp.broadcast_to(rows_right[i : i + 1, :], (8, NB))
            diagonal = pivot if i == 0 else jnp.where(sub == i, pivot, diagonal)
            solved = row_right if i == 0 else jnp.where(sub == i, row_right, solved)
            rows_left = rows_left - factor * jnp.broadcast_to(rows_left[i : i + 1, :], (8, NB))
            rows_right = rows_right - factor * row_right
        inverse_ref[8 * g : 8 * g + 8, :] = solved * lax.rsqrt(diagonal)
        if g + 1 == groups:
            break
        over = 1.0 / diagonal
        rows_left, rows_right = rows_left * over, rows_right * over
        spread_left = [jnp.broadcast_to(rows_left[i : i + 1, :], (8, NB)) for i in range(8)]
        spread_right = [jnp.broadcast_to(rows_right[i : i + 1, :], (8, NB)) for i in range(8)]
        for v in range(g + 1, groups):
            factors = [jnp.broadcast_to(left[v][:, 8 * g + i : 8 * g + i + 1], (8, NB)) for i in range(8)]
            for i in range(8):
                left[v] = left[v] - factors[i] * spread_left[i]
                right[v] = right[v] - factors[i] * spread_right[i]


def factor_blocks(front, high, low, block, inverse, count, height, emit):
    chunks = height // CHUNK
    block[...] = front[0, 0:NB, 0:NB]

    def solve(panel, pair, first):
        cols = slice(first, first + NB)
        inv_high, inv_low = split(inverse[...])

        def one(k, carry):
            rows = rows_of(k, CHUNK)
            value = times(*split(front[pair, rows, cols]), inv_high, inv_low)
            place = lax.broadcasted_iota(jnp.int32, (CHUNK, NB), 0) + (k * CHUNK - panel * NB)
            value = jnp.where(place >= lax.broadcasted_iota(jnp.int32, (CHUNK, NB), 1), value, 0.0)
            value_high, value_low = split(value)
            high[pair, rows, cols] = value_high
            low[pair, rows, cols] = value_low
            emit(panel, rows, value)
            return carry

        lax.fori_loop(panel * NB // CHUNK, chunks, one, 0)

    def step(panel, carry):
        pair = panel // 2
        block_inverse(block, inverse)

        @pl.when(panel % 2 == 0)
        def _():
            solve(panel, pair, 0)
            next_rows = rows_of(panel + 1, NB)
            part_high = high[pair, next_rows, 0:NB]
            part_low = low[pair, next_rows, 0:NB]

            def one(k, carry):
                rows = rows_of(k, CHUNK)
                front[pair, rows, NB:PAIR] -= times(
                    high[pair, rows, 0:NB], low[pair, rows, 0:NB], part_high, part_low
                )
                return carry

            lax.fori_loop(panel * NB // CHUNK, chunks, one, 0)
            block[...] = front[pair, next_rows, NB:PAIR]

        @pl.when(panel % 2 == 1)
        def _():
            solve(panel, pair, NB)

            def column(q, carry):
                part_high = high[pair, rows_of(q, PAIR), :]
                part_low = low[pair, rows_of(q, PAIR), :]

                def one(k, carry):
                    rows = rows_of(k, CHUNK)
                    front[q, rows, :] -= times(high[pair, rows, :], low[pair, rows, :], part_high, part_low)
                    return carry

                lax.fori_loop(q * PAIR // CHUNK, chunks, one, 0)
                return carry

            lax.fori_loop(pair + 1, count // 2, column, 0)

            @pl.when(pair + 1 < count // 2)
            def _():
                block[...] = front[pair + 1, rows_of(panel + 1, NB), 0:NB]

        return carry

    lax.fori_loop(0, count, step, 0)


def entry_block(entries, grid_count, row, col):
    most = grid_count // 2
    if row >= grid_count:
        at = most + 1 + row - grid_count
        return entries[col, at * NB : (at + 1) * NB, :]
    at = row - col
    if at <= most:
        return entries[col, at * NB : (at + 1) * NB, :]
    at = grid_count - at
    return entries[row, at * NB : (at + 1) * NB, :].T


def packed_at(row, col):
    return col * CB - col * (col - 1) // 2 + row - col


def masked(value, live_row, live_col, same):
    if not same:
        return jnp.where(live_row * live_col > 0, value, 0.0)
    row = lax.broadcasted_iota(jnp.int32, (NB, NB), 0)
    col = lax.broadcasted_iota(jnp.int32, (NB, NB), 1)
    kept = jnp.where(live_row * live_col > 0, value, 0.0)
    alone = jnp.where(live_row == 0, 1.0, 0.0)
    return kept + jnp.where(row == col, alone, 0.0)


def child_kernel(index, grid_count, live, place, entries, *rest):
    done = rest[: 2 * index]
    own, high, low, front, block, inverse = rest[2 * index :]
    base = index * grid_count * NB
    height = F - base
    own[...] = jnp.zeros_like(own)

    for col in range(grid_count):
        live_col = live[index * grid_count + col]
        for r in range(col, height // NB):
            front[col // 2, r * NB : (r + 1) * NB, col % 2 * NB : (col % 2 + 1) * NB] = masked(
                entry_block(entries, grid_count, r, col), live[base // NB + r], live_col, col == r
            )
    for earlier in range(index):
        past_high, past_low = done[2 * earlier], done[2 * earlier + 1]
        offset = (index - earlier) * grid_count * NB

        def column(q, carry):
            def pairs(p, carry):
                near = pl.ds(pl.multiple_of(offset + q * PAIR, PAIR), PAIR)
                part_high, part_low = past_high[p, near, :], past_low[p, near, :]

                def one(k, carry):
                    rows = pl.ds(pl.multiple_of(offset + k * CHUNK, CHUNK), CHUNK)
                    front[q, rows_of(k, CHUNK), :] -= times(
                        past_high[p, rows, :], past_low[p, rows, :], part_high, part_low
                    )
                    return carry

                return lax.fori_loop(q * PAIR // CHUNK, height // CHUNK, one, carry)

            return lax.fori_loop(0, grid_count // 2, pairs, carry)

        lax.fori_loop(0, grid_count // 2, column, 0)

    def emit(panel, rows, value):
        @pl.when(panel == place[0])
        def _():
            own[pl.ds(pl.multiple_of(rows.start + base, NB), rows.size), :] = value

    factor_blocks(front, high, low, block, inverse, grid_count, height, emit)


def product_kernel(pivot_rounds, grid_count, *rest):
    done = rest[: 2 * pivot_rounds]
    (out,) = rest[2 * pivot_rounds :]
    for q in range(CB // 2):

        def tile(k, carry):
            total = None
            for index in range(pivot_rounds):
                past_high, past_low = done[2 * index], done[2 * index + 1]
                offset = PIVOTS - index * grid_count * NB
                rows = pl.ds(pl.multiple_of(offset + k * PAIR, PAIR), PAIR)
                near = slice(offset + q * PAIR, offset + (q + 1) * PAIR)
                for p in range(grid_count // 2):
                    product = times(
                        past_high[p, rows, :], past_low[p, rows, :], past_high[p, near, :], past_low[p, near, :]
                    )
                    total = product if total is None else total + product
            for row in range(2):
                for col in range(2):
                    r = 2 * k + row
                    c = 2 * q + col

                    @pl.when(r >= c)
                    def _():
                        part = total[row * NB : (row + 1) * NB, col * NB : (col + 1) * NB]
                        out[packed_at(r, c)] = part

            return carry

        lax.fori_loop(q, CB // 2, tile, 0)


def parent_kernel(slots, grid_count, late, blocks, mine_at, other_at, *rest):
    my_entries, other_entries = rest[:late], rest[late : 2 * late]
    my_product, other_product, diagonal, out = rest[2 * late : 2 * late + 4]
    mine, other, own, front, high, low, block, inverse, sems = rest[2 * late + 4 :]
    for schur, entries, product in ((mine, my_entries, my_product), (other, other_entries, other_product)):
        for c in range(CB):
            t, inner = divmod(c, grid_count)
            for r in range(c, CB):
                at = packed_at(r, c)
                schur[at] = entry_block(entries[t], grid_count, r - t * grid_count, inner) - product[at]
    row_id = lax.broadcasted_iota(jnp.int32, (NB, NB), 0)
    col_id = lax.broadcasted_iota(jnp.int32, (NB, NB), 1)
    own[...] = jnp.zeros_like(own)

    def extension(schur, at, r, b, turn):
        cr, cb = at[r], at[b]
        present = (cr >= 0) & (cb >= 0)
        cr, cb = jnp.where(present, cr, 0), jnp.where(present, cb, 0)
        if not turn:
            value = schur[packed_at(cr, cb)]
        else:
            value = schur[packed_at(jnp.maximum(cr, cb), jnp.minimum(cr, cb))]
            value = jnp.where(cr >= cb, value, value.T)
        return jnp.where(present, value, 0.0)

    def assembled(r, b, turn):
        start = jnp.where((row_id == col_id) & (r == b), diagonal[pl.ds(b, 1), :], 0.0)
        return start + extension(mine, mine_at, r, b, turn) + extension(other, other_at, r, b, turn)

    def load(q, carry):
        for half in range(2):
            b = 2 * q + half

            def one(r, carry):
                front[q, rows_of(r, NB), half * NB : (half + 1) * NB] = assembled(r, b, False)
                return carry

            lax.fori_loop(b, FB, one, 0)
        return carry

    lax.fori_loop(0, PB // 2, load, 0)

    def emit(panel, rows, value):
        for s in range(slots):

            @pl.when(blocks[s] == panel)
            def _():
                own[s, rows, :] = value

    factor_blocks(front, high, low, block, inverse, PB, F, emit)

    def finish(s, carry):
        b = blocks[s]

        @pl.when(b >= PB)
        def _():
            def one(r, carry):
                own[s, rows_of(r, NB), :] = assembled(r, b, True)
                return carry

            lax.fori_loop(PB, FB, one, 0)
            near = rows_of(b, NB)

            def part(k, carry):
                rows = rows_of(k, CHUNK)
                total = None
                for p in range(PB // 2):
                    product = times(high[p, rows, :], low[p, rows, :], high[p, near, :], low[p, near, :])
                    total = product if total is None else total + product
                own[s, rows, :] -= total
                return carry

            lax.fori_loop(PIVOTS // CHUNK, F // CHUNK, part, 0)

        return carry

    lax.fori_loop(0, slots, finish, 0)
    copies = [pltpu.make_async_copy(own.at[s], out.at[:, s, 0, :], sems.at[s]) for s in range(slots)]
    for copy in copies:
        copy.start()
    for copy in copies:
        copy.wait()


def call(kernel, outs, scratch, smem, vmem, flops, out_space=pltpu.VMEM):
    size = sum(a.size * a.dtype.itemsize for a in vmem) + sum(a.size * a.dtype.itemsize for a in outs)
    return pl.pallas_call(
        kernel,
        out_shape=outs,
        in_specs=[SMEM] * len(smem) + [VMEM] * len(vmem),
        out_specs=[pl.BlockSpec(memory_space=out_space)] * len(outs),
        scratch_shapes=scratch,
        compiler_params=pltpu.CompilerParams(vmem_limit_bytes=LIMIT),
        cost_estimate=pl.CostEstimate(flops=flops, bytes_accessed=size, transcendentals=0),
    )(*smem, *vmem)


def shape(dims, dtype=f32):
    return jax.ShapeDtypeStruct(dims, dtype)


def body(child_front, child_live, child_map, parent_owner, parent_shift):
    grid_count = lax.axis_size("grid")
    leaf_count = lax.axis_size("leaf")
    grid_pos = lax.axis_index("grid")
    leaf_pos = lax.axis_index("leaf")
    member = leaf_pos % 2
    sibling = leaf_pos ^ 1
    rounds = child_front.shape[3]
    pivot_rounds = PIVOTS // (NB * grid_count)
    slots = parent_shift.shape[2]
    swap = [(source, source ^ 1) for source in range(leaf_count)]
    entries = child_front.reshape(F, rounds, NB)
    shifts = lax.all_gather(parent_shift.reshape(slots, NB), "grid", axis=0)
    half_ring = (grid_pos + jnp.arange(grid_count // 2 + 1)) % grid_count

    def sent(t):
        base = t * grid_count * NB
        near = entries[base : base + grid_count * NB, t, :].reshape(grid_count, NB, NB)
        near = jnp.take(near, half_ring, axis=0).reshape(-1, NB)
        return jnp.concatenate([near, entries[base + grid_count * NB :, t, :]], axis=0)

    gathered = [lax.all_gather(sent(t), "grid", axis=0) for t in range(rounds)]

    my_live = lax.dynamic_index_in_dim(child_live, leaf_pos, 0, keepdims=False)[0]
    other_live = lax.dynamic_index_in_dim(child_live, sibling, 0, keepdims=False)[0]
    my_map = lax.dynamic_index_in_dim(child_map, leaf_pos, 0, keepdims=False)[0]
    other_map = lax.dynamic_index_in_dim(child_map, sibling, 0, keepdims=False)[0]

    def sources(targets, alive):
        hit = (targets[None, :] == jnp.arange(FB)[:, None]) & (alive[None, PB:] > 0)
        return jnp.sum(jnp.where(hit, jnp.arange(1, CB + 1)[None, :], 0), axis=1).astype(jnp.int32) - 1

    owner_row = lax.dynamic_index_in_dim(parent_owner, leaf_pos // 2, 0, keepdims=False)
    slot_ids = (member * grid_count + grid_pos) * slots + jnp.arange(slots)
    holders = (owner_row[:, None] == slot_ids[None, :]).astype(jnp.int32)
    parent_blocks = jnp.sum(holders * jnp.arange(FB)[:, None], axis=0).astype(jnp.int32)
    other_shifts = lax.ppermute(shifts, "leaf", swap)
    first = jnp.where(member == 0, shifts, other_shifts)
    second = jnp.where(member == 0, other_shifts, shifts)
    by_slot = jnp.concatenate([first, second], axis=0).reshape(FB, NB)
    chosen = owner_row[:, None, None] == jnp.arange(FB)[None, :, None]
    diagonal = jnp.sum(jnp.where(chosen, by_slot[None], 0.0), axis=1)

    gathered[0], diagonal = lax.optimization_barrier((gathered[0], diagonal))
    place = grid_pos.astype(jnp.int32).reshape(1)
    owned = []
    done = []
    for t in range(pivot_rounds):
        height = F - t * grid_count * NB
        packed = (grid_count // 2, height, PAIR)
        own, high, low = call(
            functools.partial(child_kernel, t, grid_count),
            [shape((F, NB)), shape(packed, bf16), shape(packed, bf16)],
            [pltpu.VMEM(packed, f32), pltpu.VMEM((NB, NB), f32), pltpu.VMEM((NB, NB), f32)],
            [my_live, place],
            [gathered[t], *done],
            25_000_000_000,
        )
        owned.append(own)
        done += [high, low]
    late = gathered[pivot_rounds:]
    lower = CB * (CB + 1) // 2
    (mine,) = call(
        functools.partial(product_kernel, pivot_rounds, grid_count),
        [shape((lower, NB, NB))],
        [],
        [],
        done,
        6_000_000_000,
    )
    other = lax.ppermute(mine, "leaf", swap)
    other_late = [lax.ppermute(part, "leaf", swap) for part in late]
    packed = (PB // 2, F, PAIR)
    (parent,) = call(
        functools.partial(parent_kernel, slots, grid_count, len(late)),
        [shape((F, slots, 1, NB))],
        [
            pltpu.VMEM((lower, NB, NB), f32),
            pltpu.VMEM((lower, NB, NB), f32),
            pltpu.VMEM((slots, F, NB), f32),
            pltpu.VMEM(packed, f32),
            pltpu.VMEM(packed, bf16),
            pltpu.VMEM(packed, bf16),
            pltpu.VMEM((NB, NB), f32),
            pltpu.VMEM((NB, NB), f32),
            pltpu.SemaphoreType.DMA((slots,)),
        ],
        [parent_blocks, sources(my_map, my_live), sources(other_map, other_live)],
        [*late, *other_late, mine, other, diagonal],
        50_000_000_000,
        pl.ANY,
    )
    child_factor = jnp.stack(owned, axis=1)
    return (
        child_factor.reshape(1, 1, F, pivot_rounds, 1, NB),
        parent.reshape(1, 1, F, slots, 1, NB),
    )


def solution(mesh):
    in_specs = (
        P("leaf", None, None, None, "grid", None),
        P(),
        P(),
        P(),
        P("leaf", None, None, "grid", None),
    )
    out_specs = (
        P("leaf", None, None, None, "grid", None),
        P("leaf", None, None, None, "grid", None),
    )
    return jax.shard_map(body, mesh=mesh, in_specs=in_specs, out_specs=out_specs, check_vma=False)
```

```python
import functools

import jax
import jax.numpy as jnp
from jax import lax
from jax.experimental import pallas as pl
from jax.experimental.pallas import tpu as pltpu
from jax.sharding import PartitionSpec as P

F = 2048
PIVOTS = 1024
NB = 128
FB = 16
PB = 8
CB = 8
CHUNK = 512
PAIR = 256
f32 = jnp.float32
bf16 = jnp.bfloat16
NT = (((1,), (1,)), ((), ()))
VMEM = pl.BlockSpec(memory_space=pltpu.VMEM)
SMEM = pl.BlockSpec(memory_space=pltpu.SMEM)
LIMIT = 56 * 1024 * 1024


def split(value):
    high = value.astype(bf16)
    return high, (value - high.astype(f32)).astype(bf16)


def times(a_high, a_low, b_high, b_low):
    def dot(a, b):
        return lax.dot_general(a, b, NT, preferred_element_type=f32)

    return dot(a_high, b_high) + (dot(a_low, b_high) + dot(a_high, b_low))


def rows_of(index, count):
    return pl.ds(pl.multiple_of(index * count, count), count)


def block_inverse(block_ref, inverse_ref):
    lane = lax.broadcasted_iota(jnp.int32, (8, NB), 1)
    sub = lax.broadcasted_iota(jnp.int32, (8, NB), 0)
    groups = NB // 8
    left = [block_ref[8 * g : 8 * g + 8, :] for g in range(groups)]
    right = [jnp.where(lane == sub + 8 * g, 1.0, 0.0).astype(f32) for g in range(groups)]
    for g in range(groups):
        columns = [jnp.broadcast_to(left[g][:, 8 * g + i : 8 * g + i + 1], (8, NB)) for i in range(8)]
        rows_left, rows_right = left[g], right[g]
        diagonal = solved = None
        for i in range(8):
            pivot = jnp.broadcast_to(columns[i][i : i + 1, :], (8, NB))
            factor = jnp.where(sub == i, 0.0, columns[i]) * (1.0 / pivot)
            for c in range(i + 1, 8):
                columns[c] = columns[c] - factor * jnp.broadcast_to(columns[c][i : i + 1, :], (8, NB))
            row_right = jnp.broadcast_to(rows_right[i : i + 1, :], (8, NB))
            diagonal = pivot if i == 0 else jnp.where(sub == i, pivot, diagonal)
            solved = row_right if i == 0 else jnp.where(sub == i, row_right, solved)
            rows_left = rows_left - factor * jnp.broadcast_to(rows_left[i : i + 1, :], (8, NB))
            rows_right = rows_right - factor * row_right
        inverse_ref[8 * g : 8 * g + 8, :] = solved * lax.rsqrt(diagonal)
        if g + 1 == groups:
            break
        over = 1.0 / diagonal
        rows_left, rows_right = rows_left * over, rows_right * over
        spread_left = [jnp.broadcast_to(rows_left[i : i + 1, :], (8, NB)) for i in range(8)]
        spread_right = [jnp.broadcast_to(rows_right[i : i + 1, :], (8, NB)) for i in range(8)]
        for v in range(g + 1, groups):
            factors = [jnp.broadcast_to(left[v][:, 8 * g + i : 8 * g + i + 1], (8, NB)) for i in range(8)]
            for i in range(8):
                left[v] = left[v] - factors[i] * spread_left[i]
                right[v] = right[v] - factors[i] * spread_right[i]


def factor_blocks(front, high, low, block, inverse, count, height, emit):
    chunks = height // CHUNK
    block[...] = front[0, 0:NB, 0:NB]

    def solve(panel, pair, first):
        cols = slice(first, first + NB)
        inv_high, inv_low = split(inverse[...])

        def one(k, carry):
            rows = rows_of(k, CHUNK)
            value = times(*split(front[pair, rows, cols]), inv_high, inv_low)
            place = lax.broadcasted_iota(jnp.int32, (CHUNK, NB), 0) + (k * CHUNK - panel * NB)
            value = jnp.where(place >= lax.broadcasted_iota(jnp.int32, (CHUNK, NB), 1), value, 0.0)
            value_high, value_low = split(value)
            high[pair, rows, cols] = value_high
            low[pair, rows, cols] = value_low
            emit(panel, rows, value)
            return carry

        lax.fori_loop(panel * NB // CHUNK, chunks, one, 0)

    def step(panel, carry):
        pair = panel // 2
        block_inverse(block, inverse)

        @pl.when(panel % 2 == 0)
        def _():
            solve(panel, pair, 0)
            next_rows = rows_of(panel + 1, NB)
            part_high = high[pair, next_rows, 0:NB]
            part_low = low[pair, next_rows, 0:NB]

            def one(k, carry):
                rows = rows_of(k, CHUNK)
                front[pair, rows, NB:PAIR] -= times(
                    high[pair, rows, 0:NB], low[pair, rows, 0:NB], part_high, part_low
                )
                return carry

            lax.fori_loop(panel * NB // CHUNK, chunks, one, 0)
            block[...] = front[pair, next_rows, NB:PAIR]

        @pl.when(panel % 2 == 1)
        def _():
            solve(panel, pair, NB)

            def column(q, carry):
                part_high = high[pair, rows_of(q, PAIR), :]
                part_low = low[pair, rows_of(q, PAIR), :]

                def one(k, carry):
                    rows = rows_of(k, CHUNK)
                    front[q, rows, :] -= times(high[pair, rows, :], low[pair, rows, :], part_high, part_low)
                    return carry

                lax.fori_loop(q * PAIR // CHUNK, chunks, one, 0)
                return carry

            lax.fori_loop(pair + 1, count // 2, column, 0)

            @pl.when(pair + 1 < count // 2)
            def _():
                block[...] = front[pair + 1, rows_of(panel + 1, NB), 0:NB]

        return carry

    lax.fori_loop(0, count, step, 0)


def entry_block(entries, grid_count, row, col, first=0):
    most = grid_count // 2
    if row >= grid_count:
        at = first + most + 1 + row - grid_count
        return entries[col, at * NB : (at + 1) * NB, :]
    at = row - col
    if at <= most:
        at += first
        return entries[col, at * NB : (at + 1) * NB, :]
    at = first + grid_count - at
    return entries[row, at * NB : (at + 1) * NB, :].T


def packed_at(row, col):
    return col * CB - col * (col - 1) // 2 + row - col


def masked(value, live_row, live_col, same):
    if not same:
        return jnp.where(live_row * live_col > 0, value, 0.0)
    row = lax.broadcasted_iota(jnp.int32, (NB, NB), 0)
    col = lax.broadcasted_iota(jnp.int32, (NB, NB), 1)
    kept = jnp.where(live_row * live_col > 0, value, 0.0)
    alone = jnp.where(live_row == 0, 1.0, 0.0)
    return kept + jnp.where(row == col, alone, 0.0)


def child_kernel(index, grid_count, live, place, entries, *rest):
    done = rest[: 2 * index]
    own, high, low, front, block, inverse = rest[2 * index :]
    base = index * grid_count * NB
    height = F - base
    own[...] = jnp.zeros_like(own)

    for col in range(grid_count):
        live_col = live[index * grid_count + col]
        for r in range(col, height // NB):
            front[col // 2, r * NB : (r + 1) * NB, col % 2 * NB : (col % 2 + 1) * NB] = masked(
                entry_block(entries, grid_count, r, col), live[base // NB + r], live_col, col == r
            )
    for earlier in range(index):
        past_high, past_low = done[2 * earlier], done[2 * earlier + 1]
        offset = (index - earlier) * grid_count * NB

        def column(q, carry):
            def pairs(p, carry):
                near = pl.ds(pl.multiple_of(offset + q * PAIR, PAIR), PAIR)
                part_high, part_low = past_high[p, near, :], past_low[p, near, :]

                def one(k, carry):
                    rows = pl.ds(pl.multiple_of(offset + k * CHUNK, CHUNK), CHUNK)
                    front[q, rows_of(k, CHUNK), :] -= times(
                        past_high[p, rows, :], past_low[p, rows, :], part_high, part_low
                    )
                    return carry

                return lax.fori_loop(q * PAIR // CHUNK, height // CHUNK, one, carry)

            return lax.fori_loop(0, grid_count // 2, pairs, carry)

        lax.fori_loop(0, grid_count // 2, column, 0)

    def emit(panel, rows, value):
        @pl.when(panel == place[0])
        def _():
            own[pl.ds(pl.multiple_of(rows.start + base, NB), rows.size), :] = value

    factor_blocks(front, high, low, block, inverse, grid_count, height, emit)


def product_kernel(pivot_rounds, grid_count, *rest):
    done = rest[: 2 * pivot_rounds]
    (out,) = rest[2 * pivot_rounds :]
    for q in range(CB // 2):

        def tile(k, carry):
            total = None
            for index in range(pivot_rounds):
                past_high, past_low = done[2 * index], done[2 * index + 1]
                offset = PIVOTS - index * grid_count * NB
                rows = pl.ds(pl.multiple_of(offset + k * PAIR, PAIR), PAIR)
                near = slice(offset + q * PAIR, offset + (q + 1) * PAIR)
                for p in range(grid_count // 2):
                    product = times(
                        past_high[p, rows, :], past_low[p, rows, :], past_high[p, near, :], past_low[p, near, :]
                    )
                    total = product if total is None else total + product
            for row in range(2):
                for col in range(2):
                    r = 2 * k + row
                    c = 2 * q + col

                    @pl.when(r >= c)
                    def _():
                        part = total[row * NB : (row + 1) * NB, col * NB : (col + 1) * NB]
                        out[packed_at(r, c)] = part

            return carry

        lax.fori_loop(q, CB // 2, tile, 0)


def parent_kernel(slots, grid_count, firsts, blocks, mine_at, other_at, *rest):
    my_entries, other_entries, my_product, other_product, diagonal = rest[:5]
    owned = rest[5 : len(rest) - 11]
    out, child_out, mine, other, own, front, high, low, block, inverse, sems = rest[len(rest) - 11 :]
    child_copies = [
        pltpu.make_async_copy(part, child_out.at[:, t, 0, :], sems.at[slots + t]) for t, part in enumerate(owned)
    ]
    for copy in child_copies:
        copy.start()
    for schur, entries, product in ((mine, my_entries, my_product), (other, other_entries, other_product)):
        for c in range(CB):
            t, inner = divmod(c, grid_count)
            for r in range(c, CB):
                at = packed_at(r, c)
                schur[at] = entry_block(
                    entries, grid_count, r - t * grid_count, inner, firsts[t]
                ) - product[at]
    row_id = lax.broadcasted_iota(jnp.int32, (NB, NB), 0)
    col_id = lax.broadcasted_iota(jnp.int32, (NB, NB), 1)
    own[...] = jnp.zeros_like(own)

    def extension(schur, at, r, b, turn):
        cr, cb = at[r], at[b]
        present = (cr >= 0) & (cb >= 0)
        cr, cb = jnp.where(present, cr, 0), jnp.where(present, cb, 0)
        if not turn:
            value = schur[packed_at(cr, cb)]
        else:
            value = schur[packed_at(jnp.maximum(cr, cb), jnp.minimum(cr, cb))]
            value = jnp.where(cr >= cb, value, value.T)
        return jnp.where(present, value, 0.0)

    def assembled(r, b, turn):
        start = jnp.where((row_id == col_id) & (r == b), diagonal[pl.ds(b, 1), :], 0.0)
        return start + extension(mine, mine_at, r, b, turn) + extension(other, other_at, r, b, turn)

    def load(q, carry):
        for half in range(2):
            b = 2 * q + half

            def one(r, carry):
                front[q, rows_of(r, NB), half * NB : (half + 1) * NB] = assembled(r, b, False)
                return carry

            lax.fori_loop(b, FB, one, 0)
        return carry

    lax.fori_loop(0, PB // 2, load, 0)

    def emit(panel, rows, value):
        for s in range(slots):

            @pl.when(blocks[s] == panel)
            def _():
                own[s, rows, :] = value

    factor_blocks(front, high, low, block, inverse, PB, F, emit)

    def finish(s, carry):
        b = blocks[s]

        @pl.when(b >= PB)
        def _():
            def one(r, carry):
                own[s, rows_of(r, NB), :] = assembled(r, b, True)
                return carry

            lax.fori_loop(PB, FB, one, 0)
            near = rows_of(b, NB)

            def part(k, carry):
                rows = rows_of(k, CHUNK)
                total = None
                for p in range(PB // 2):
                    product = times(high[p, rows, :], low[p, rows, :], high[p, near, :], low[p, near, :])
                    total = product if total is None else total + product
                own[s, rows, :] -= total
                return carry

            lax.fori_loop(PIVOTS // CHUNK, F // CHUNK, part, 0)

        return carry

    lax.fori_loop(0, slots, finish, 0)
    copies = [pltpu.make_async_copy(own.at[s], out.at[:, s, 0, :], sems.at[s]) for s in range(slots)]
    for copy in copies:
        copy.start()
    for copy in copies + child_copies:
        copy.wait()


def call(kernel, outs, scratch, smem, vmem, flops, out_space=pltpu.VMEM, passed=()):
    size = sum(a.size * a.dtype.itemsize for a in vmem) + sum(a.size * a.dtype.itemsize for a in outs)
    return pl.pallas_call(
        kernel,
        out_shape=outs,
        in_specs=[SMEM] * len(smem) + [VMEM] * len(vmem) + [pl.BlockSpec(memory_space=pl.ANY)] * len(passed),
        out_specs=[pl.BlockSpec(memory_space=out_space)] * len(outs),
        scratch_shapes=scratch,
        compiler_params=pltpu.CompilerParams(vmem_limit_bytes=LIMIT),
        cost_estimate=pl.CostEstimate(flops=flops, bytes_accessed=size, transcendentals=0),
    )(*smem, *vmem, *passed)


def shape(dims, dtype=f32):
    return jax.ShapeDtypeStruct(dims, dtype)


def body(child_front, child_live, child_map, parent_owner, parent_shift):
    grid_count = lax.axis_size("grid")
    leaf_count = lax.axis_size("leaf")
    grid_pos = lax.axis_index("grid")
    leaf_pos = lax.axis_index("leaf")
    member = leaf_pos % 2
    sibling = leaf_pos ^ 1
    rounds = child_front.shape[3]
    pivot_rounds = PIVOTS // (NB * grid_count)
    slots = parent_shift.shape[2]
    swap = [(source, source ^ 1) for source in range(leaf_count)]
    entries = child_front.reshape(F, rounds, NB)
    shifts = lax.all_gather(parent_shift.reshape(slots, NB), "grid", axis=0)
    half_ring = (grid_pos + jnp.arange(grid_count // 2 + 1)) % grid_count

    def sent(t):
        base = t * grid_count * NB
        near = entries[base : base + grid_count * NB, t, :].reshape(grid_count, NB, NB)
        near = jnp.take(near, half_ring, axis=0).reshape(-1, NB)
        return jnp.concatenate([near, entries[base + grid_count * NB :, t, :]], axis=0)

    gathered = [lax.all_gather(sent(t), "grid", axis=0) for t in range(pivot_rounds)]
    late_sent = [sent(t) for t in range(pivot_rounds, rounds)]
    firsts = [sum(part.shape[0] for part in late_sent[:t]) // NB for t in range(len(late_sent))]
    late = lax.all_gather(jnp.concatenate(late_sent, axis=0), "grid", axis=0)

    my_live = lax.dynamic_index_in_dim(child_live, leaf_pos, 0, keepdims=False)[0]
    other_live = lax.dynamic_index_in_dim(child_live, sibling, 0, keepdims=False)[0]
    my_map = lax.dynamic_index_in_dim(child_map, leaf_pos, 0, keepdims=False)[0]
    other_map = lax.dynamic_index_in_dim(child_map, sibling, 0, keepdims=False)[0]

    def sources(targets, alive):
        hit = (targets[None, :] == jnp.arange(FB)[:, None]) & (alive[None, PB:] > 0)
        return jnp.sum(jnp.where(hit, jnp.arange(1, CB + 1)[None, :], 0), axis=1).astype(jnp.int32) - 1

    owner_row = lax.dynamic_index_in_dim(parent_owner, leaf_pos // 2, 0, keepdims=False)
    slot_ids = (member * grid_count + grid_pos) * slots + jnp.arange(slots)
    holders = (owner_row[:, None] == slot_ids[None, :]).astype(jnp.int32)
    parent_blocks = jnp.sum(holders * jnp.arange(FB)[:, None], axis=0).astype(jnp.int32)
    other_shifts = lax.ppermute(shifts, "leaf", swap)
    first = jnp.where(member == 0, shifts, other_shifts)
    second = jnp.where(member == 0, other_shifts, shifts)
    by_slot = jnp.concatenate([first, second], axis=0).reshape(FB, NB)
    chosen = owner_row[:, None, None] == jnp.arange(FB)[None, :, None]
    diagonal = jnp.sum(jnp.where(chosen, by_slot[None], 0.0), axis=1)

    gathered[0], diagonal = lax.optimization_barrier((gathered[0], diagonal))
    place = grid_pos.astype(jnp.int32).reshape(1)
    owned = []
    done = []
    for t in range(pivot_rounds):
        height = F - t * grid_count * NB
        packed = (grid_count // 2, height, PAIR)
        own, high, low = call(
            functools.partial(child_kernel, t, grid_count),
            [shape((F, NB)), shape(packed, bf16), shape(packed, bf16)],
            [pltpu.VMEM(packed, f32), pltpu.VMEM((NB, NB), f32), pltpu.VMEM((NB, NB), f32)],
            [my_live, place],
            [gathered[t], *done],
            25_000_000_000,
        )
        owned.append(own)
        done += [high, low]
    lower = CB * (CB + 1) // 2
    (mine,) = call(
        functools.partial(product_kernel, pivot_rounds, grid_count),
        [shape((lower, NB, NB))],
        [],
        [],
        done,
        6_000_000_000,
    )
    other = lax.ppermute(mine, "leaf", swap)
    other_late = lax.ppermute(late, "leaf", swap)
    packed = (PB // 2, F, PAIR)
    parent, child_factor = call(
        functools.partial(parent_kernel, slots, grid_count, firsts),
        [shape((F, slots, 1, NB)), shape((F, pivot_rounds, 1, NB))],
        [
            pltpu.VMEM((lower, NB, NB), f32),
            pltpu.VMEM((lower, NB, NB), f32),
            pltpu.VMEM((slots, F, NB), f32),
            pltpu.VMEM(packed, f32),
            pltpu.VMEM(packed, bf16),
            pltpu.VMEM(packed, bf16),
            pltpu.VMEM((NB, NB), f32),
            pltpu.VMEM((NB, NB), f32),
            pltpu.SemaphoreType.DMA((slots + pivot_rounds,)),
        ],
        [parent_blocks, sources(my_map, my_live), sources(other_map, other_live)],
        [late, other_late, mine, other, diagonal],
        50_000_000_000,
        pl.ANY,
        owned,
    )
    return (
        child_factor.reshape(1, 1, F, pivot_rounds, 1, NB),
        parent.reshape(1, 1, F, slots, 1, NB),
    )


def solution(mesh):
    in_specs = (
        P("leaf", None, None, None, "grid", None),
        P(),
        P(),
        P(),
        P("leaf", None, None, "grid", None),
    )
    out_specs = (
        P("leaf", None, None, None, "grid", None),
        P("leaf", None, None, None, "grid", None),
    )
    return jax.shard_map(body, mesh=mesh, in_specs=in_specs, out_specs=out_specs, check_vma=False)
```
